128 devices in a mesh: crop: 2 (over x_hi), row: 16 (over z, y), col: 4 (over x_lo, core).
Axes of the slice: x: 4 (x_hi: 2, x_lo: 2; x = x_hi * 2 + x_lo), y: 4, z: 4, core: 2. Of those that a mesh axis runs over, the one named last changes fastest.
Arguments:
- pair_state: bfloat16 [1024, 512, 128], P(('crop', 'row'), 'col'), parts along dimension 0, may hold values from -6 to 6
- valid_tokens: int32 [2], P('crop'), parts along dimension 0, may hold values from 256 to 512
- w_query: bfloat16 [128, 128], replicated, may hold values from -2 to 2
- w_key: bfloat16 [128, 128], replicated, may hold values from -2 to 2
- w_value: bfloat16 [128, 128], replicated, may hold values from -0.5 to 0.5
- w_gate: bfloat16 [128, 128], replicated, may hold values from -0.5 to 0.5
- b_gate: float32 [128], replicated, may hold values from -4 to 4
- w_bias: bfloat16 [128, 4], replicated, may hold values from -0.5 to 0.5
- w_out: bfloat16 [128, 128], replicated, may hold values from -0.5 to 0.5
- b_out: float32 [128], replicated, may hold values from -3 to 3
Outputs:
- pair_out: bfloat16 [1024, 512, 128], P(('crop', 'row'), 'col'), parts along dimension 0
The draws below stay inside these ranges and needn't reach their ends.
There are 2 independent parts, one for each index of `crop`. The reference program is written for one: setup_inputs(seed, part) draws one part's arguments, and reference() takes and returns one part's arrays. A program takes and returns all parts, laid end to end along the dimension named above; an argument that names none is the same for every part. Nothing has to cross between parts.
Inputs may be any that keep to these rules, and one draw needn't show every extreme that they name: `valid_tokens`: number of tokens of the crop that are real; the others are padding.
All inputs are finite; a program needn't handle non-finite values.
Results may differ from the reference program's by a relative error of at most 0.0055.
Values may be sent and summed in bfloat16 or wider, within the bound.
No kernel may reach another device: no remote copies, remote signals or barrier semaphores. Data moves between devices by JAX's collectives and lax.ppermute only.
A program may use at most 256 MiB of HBM per device.

```python
import jax
import jax.numpy as jnp
from jax import lax

C = 128
H = 4
D = 32
BLOCK = 8
TOKENS = 512


def drawn_weight(key):
    return jnp.clip(jax.random.normal(key, (C, C), jnp.float32), -4.0, 4.0) * C ** (-0.5)


def draw_w_query(key, part):
    key = jax.random.fold_in(key, 7)
    base = drawn_weight(key)
    return base.astype(jnp.bfloat16)


def draw_w_key(key, part):
    key = jax.random.fold_in(key, 9)
    base = drawn_weight(key)
    return base.astype(jnp.bfloat16)


def steps_of(rng, extent, split, smallest, top_value):
    def one(axis_at, blocks):
        draws = jax.random.uniform(jax.random.fold_in(jax.random.fold_in(rng, 6), axis_at), (blocks,), jnp.float32, smallest / len(split), top_value / len(split))
        return jnp.repeat(jnp.exp(draws), extent[axis_at] // blocks).reshape((-1,) + (1,) * (len(extent) - axis_at - 1))

    loudness = one(*split[0])
    for cut in split[1:]:
        loudness = loudness * one(*cut)
    return loudness


def centred(stream_key, dims, spread, limit, cuts=(), held_as=jnp.bfloat16):
    drawn = spread * jax.random.normal(stream_key, dims, jnp.float32)
    if cuts:
        drawn = drawn * steps_of(stream_key, dims, cuts, -0.22, 0.18)
    return jnp.clip(drawn, -limit, limit).astype(held_as)


def setup_inputs(seed: int = 0, part: int = 0) -> dict:
    keys = jax.random.split(jax.random.key(seed), 11)
    part_splits = jax.random.split(jax.random.fold_in(keys[10], part), 11)
    return {
        "pair_state": centred(part_splits[0], (TOKENS, TOKENS, C), 1.0, 6.0, ((0, 16), (1, 4))),
        "valid_tokens": jax.random.randint(part_splits[1], (1,), TOKENS // 2, TOKENS + 1).astype(jnp.int32),
        "w_query": draw_w_query(jax.random.fold_in(keys[10], 71), part),
        "w_key": draw_w_key(jax.random.fold_in(keys[10], 71), part),
        "w_value": centred(keys[4], (C, C), C ** -0.5, 0.5),
        "w_gate": centred(keys[5], (C, C), C ** -0.5, 0.5),
        "b_gate": centred(keys[6], (C,), 1.0, 4.0, (), jnp.float32),
        "w_bias": centred(keys[7], (C, H), C ** -0.5, 0.5),
        "w_out": centred(keys[8], (C, C), C ** -0.5, 0.5),
        "b_out": centred(keys[9], (C,), 0.5, 3.0, (), jnp.float32),
    }


MASKED_SCORE = -1000000000.0

def normalize(tensor):
    floats = tensor.astype(jnp.float32)
    average = lax.optimization_barrier(jnp.mean(floats, axis=-1, keepdims=True))
    centered = floats - average
    variance = lax.optimization_barrier(jnp.mean(centered * centered, axis=-1, keepdims=True))
    return (centered * lax.rsqrt(variance + 1e-05)).astype(jnp.bfloat16)

def reference(pair_state, valid_tokens, w_query, w_key, w_value, w_gate, b_gate, w_bias, w_out, b_out):
    normed = normalize(pair_state)
    queries = (jnp.dot(normed, w_query, preferred_element_type=jnp.float32) * D ** (-0.5)).astype(jnp.bfloat16)
    key_tiles = jnp.dot(normed, w_key, preferred_element_type=jnp.float32).astype(jnp.bfloat16)
    values = jnp.dot(normed, w_value, preferred_element_type=jnp.float32).astype(jnp.bfloat16)
    pair_bias = jnp.dot(normed, w_bias, preferred_element_type=jnp.float32).astype(jnp.bfloat16)
    bias_hik = jnp.transpose(pair_bias, (2, 1, 0)).astype(jnp.float32)
    token_ok = jnp.arange(TOKENS) < valid_tokens[0]

    def column_block(first_column):
        first_column = first_column.astype(jnp.int32)
        query_block = lax.dynamic_slice_in_dim(queries, first_column, BLOCK, 1).reshape(TOKENS, BLOCK, H, D).astype(jnp.float32)
        key_block = lax.dynamic_slice_in_dim(key_tiles, first_column, BLOCK, 1).reshape(TOKENS, BLOCK, H, D).astype(jnp.float32)
        value_block = lax.dynamic_slice_in_dim(values, first_column, BLOCK, 1).reshape(TOKENS, BLOCK, H, D).astype(jnp.float32)
        column_ok = lax.dynamic_slice_in_dim(token_ok, first_column, BLOCK, 0)
        scores = jnp.einsum('ijhd,kjhd->jhik', query_block, key_block) + bias_hik[None]
        allowed = (column_ok[:, None] & token_ok[None, :])[:, None, None, :]
        scores = jnp.where(allowed, scores, MASKED_SCORE)
        largest = lax.optimization_barrier(jnp.max(scores, axis=-1, keepdims=True))
        weights = jnp.exp(scores - largest)
        totals = lax.optimization_barrier(jnp.sum(weights, axis=-1))
        rounded = lax.optimization_barrier(weights.astype(jnp.bfloat16)).astype(jnp.float32)
        attended = jnp.einsum('jhik,kjhd->ijhd', rounded, value_block) / jnp.transpose(totals, (2, 0, 1))[..., None]
        normed_block = lax.dynamic_slice_in_dim(normed, first_column, BLOCK, 1)
        gate_value = jax.nn.sigmoid(jnp.dot(normed_block, w_gate, preferred_element_type=jnp.float32) + b_gate)
        gated_mix = (gate_value * attended.reshape(TOKENS, BLOCK, C)).astype(jnp.bfloat16)
        update = jnp.dot(gated_mix, w_out, preferred_element_type=jnp.float32) + b_out
        pair_block = lax.dynamic_slice_in_dim(pair_state, first_column, BLOCK, 1).astype(jnp.float32)
        return (pair_block + update).astype(jnp.bfloat16)
    blocks_out = lax.map(column_block, jnp.arange(0, TOKENS, BLOCK, dtype=jnp.int32))
    return jnp.transpose(blocks_out, (1, 0, 2, 3)).reshape(TOKENS, TOKENS, C)
```

```python
import functools

import jax
import jax.numpy as jnp
from jax import lax
from jax.experimental import pallas as pl
from jax.experimental.pallas import tpu as pltpu
from jax.sharding import Mesh
from jax.sharding import PartitionSpec as P

F32 = jnp.float32
BF16 = jnp.bfloat16
MASKED_SCORE = -1000000000.0
CONTRACT_LAST = (((1,), (1,)), ((), ()))


def normalize(floats):
    average = jnp.mean(floats, axis=-1, keepdims=True)
    centered = floats - average
    variance = jnp.mean(centered * centered, axis=-1, keepdims=True)
    return (centered * lax.rsqrt(variance + 1e-05)).astype(BF16)


def pack_kernel(x_ref, wb_ref, out_ref):
    rows, cols, channels = x_ref.shape
    peers, slots = out_ref.shape[:2]
    heads = wb_ref.shape[0]
    picks = slots - heads
    bias = []
    for r in range(rows):
        normed = normalize(x_ref[r].astype(F32))
        bias.append(
            lax.dot_general(wb_ref[...], normed, CONTRACT_LAST, preferred_element_type=F32)
        )
    bias = jnp.stack(bias, axis=1).astype(BF16)
    for d in range(peers):
        out_ref[d, picks:] = bias
    turned = jnp.swapaxes(x_ref[...], 0, 1)
    for q in range(picks):
        out_ref[:, q] = turned[q * peers : (q + 1) * peers]


def bias_kernel(info_ref, got_ref, out_ref):
    rows, _, heads, tile_rows, width = got_ref.shape
    tokens = rows * tile_rows
    valid = info_ref[2]
    key_ok = lax.broadcasted_iota(jnp.int32, (1, tokens), 1) < valid
    for h in range(heads):
        block = got_ref[:, 0, h].reshape(tokens, width).astype(F32)
        out_ref[h, 0] = jnp.where(key_ok, jnp.transpose(block), MASKED_SCORE).astype(BF16)


def attend_kernel(
    info_ref, x_ref, own_ref, other_ref, wq_ref, wk_ref, wv_ref, wg_ref, bg_ref, wo_ref, bo_ref,
    out_ref, q_s, g_s,
):
    core, peer, valid = info_ref[0], info_ref[1], info_ref[2]
    rows, _, _, tile_rows, channels = x_ref.shape
    tokens = rows * tile_rows
    heads = own_ref.shape[0]
    head_size = channels // heads
    width = own_ref.shape[2]
    blocks = width // tile_rows
    column = (pl.program_id(0) * 2 + core) * width + pl.program_id(1) * 32 + peer
    normed = normalize(x_ref[...].reshape(tokens, channels).astype(F32))
    values = jnp.dot(normed, wv_ref[...], preferred_element_type=F32).astype(BF16)
    g_s[...] = jax.nn.sigmoid(
        jnp.dot(normed, wg_ref[...], preferred_element_type=F32) + bg_ref[...]
    )
    lane_head = lax.broadcasted_iota(jnp.int32, (1, channels), 1) // head_size

    def finish(at, attended):
        mix = (g_s[pl.ds(at, width), :] * attended).astype(BF16)
        update = jnp.dot(mix, wo_ref[...], preferred_element_type=F32) + bo_ref[...]
        tile = pl.ds(at // tile_rows, blocks)
        mine = x_ref[tile].reshape(width, channels).astype(F32)
        out_ref[tile] = (mine + update).astype(BF16).reshape(blocks, 1, 1, tile_rows, channels)

    @pl.when(column < valid)
    def _():
        q_s[...] = (
            jnp.dot(normed, wq_ref[...], preferred_element_type=F32) * head_size ** (-0.5)
        ).astype(BF16)
        keys = jnp.dot(normed, wk_ref[...], preferred_element_type=F32).astype(BF16)
        values_ones = jnp.concatenate([values, jnp.ones_like(values)], axis=1)
        starts = [
            pl.multiple_of((xl * 2 + c) * width, width) for c in (core, 1 - core) for xl in (0, 1)
        ]
        queries = jnp.concatenate([q_s[pl.ds(at, width), :] for at in starts], axis=0)
        top = total = None
        for h in range(heads):
            picked = jnp.where(lane_head == h, queries, jnp.zeros_like(queries))
            scores = lax.dot_general(picked, keys, CONTRACT_LAST, preferred_element_type=F32)
            bias = jnp.concatenate(
                [own_ref[h].reshape(2 * width, tokens), other_ref[h].reshape(2 * width, tokens)],
                axis=0,
            )
            scores = scores + bias.astype(F32)
            weights = jnp.exp(scores - jnp.max(scores, axis=1, keepdims=True)).astype(BF16)
            both = jnp.dot(weights, values_ones, preferred_element_type=F32)
            if h == 0:
                top, total = both[:, :channels], both[:, channels:]
            else:
                top = jnp.where(lane_head == h, both[:, :channels], top)
                total = jnp.where(lane_head == h, both[:, channels:], total)
        attended = top / total
        for n, at in enumerate(starts):
            finish(at, attended[n * width : (n + 1) * width])

    @pl.when(column >= valid)
    def _():
        uniform = jnp.mean(values.astype(F32), axis=0, keepdims=True)
        for n in range(tokens // width):
            finish(n * width, jnp.broadcast_to(uniform, (width, channels)))


def unpack_kernel(got_ref, out_ref):
    peers, picks = got_ref.shape[:2]
    for q in range(picks):
        out_ref[:, q * peers : (q + 1) * peers] = jnp.swapaxes(got_ref[:, q], 0, 1)


def call(kernel, name, out, *operands, grid=None, in_specs=None, out_specs=None, scratch=()):
    whole = pl.BlockSpec(memory_space=pltpu.VMEM)
    extra = {} if grid is None else {"grid": grid}
    return pl.pallas_call(
        kernel,
        out_shape=jax.ShapeDtypeStruct(out, BF16),
        in_specs=in_specs or [whole] * len(operands),
        out_specs=out_specs or whole,
        scratch_shapes=list(scratch),
        compiler_params=pltpu.CompilerParams(vmem_limit_bytes=48 << 20),
        name=name,
        **extra,
    )(*operands)


def local(pair_state, valid_tokens, w_query, w_key, w_value, w_gate, b_gate, w_bias, w_out, b_out):
    tile_rows, tile_cols, channels = pair_state.shape
    heads = w_bias.shape[1]
    rows, pairs = lax.axis_size("row"), lax.axis_size("xl")
    peers = rows * pairs
    picks = tile_cols // peers
    tokens = rows * tile_rows
    core = lax.axis_index("core")
    peer = lax.axis_index("row") * pairs + lax.axis_index("xl")
    info = jnp.stack([core, peer, valid_tokens[0]]).astype(jnp.int32)
    smem = pl.BlockSpec(memory_space=pltpu.SMEM)

    sent = call(
        pack_kernel, "pack", (peers, picks + heads, tile_rows, channels), pair_state, w_bias.T
    )
    got = lax.all_to_all(sent, ("row", "xl"), 0, 0, tiled=True)
    got = got.reshape(rows, pairs, picks + heads, tile_rows, channels)
    own = call(
        bias_kernel, "turn_bias", (heads, pairs, tile_cols, tokens), info, got,
        grid=(pairs,),
        in_specs=[
            smem,
            pl.BlockSpec((rows, 1, heads, tile_rows, channels), lambda a: (0, a, 1, 0, 0)),
        ],
        out_specs=pl.BlockSpec((heads, 1, tile_cols, tokens), lambda a: (0, a, 0, 0)),
    )
    other = lax.ppermute(own, "core", [(0, 1), (1, 0)])
    column = pl.BlockSpec((rows, 1, 1, tile_rows, channels), lambda a, b: (0, a, b, 0, 0))

    def fixed(array):
        return pl.BlockSpec(array.shape, lambda a, b: (0,) * array.ndim)

    operands = [own, other, w_query, w_key, w_value, w_gate, b_gate[None], w_out, b_out[None]]
    done = call(
        attend_kernel, "attend", (rows, pairs, picks, tile_rows, channels), info, got, *operands,
        grid=(pairs, picks),
        in_specs=[smem, column] + [fixed(array) for array in operands],
        out_specs=column,
        scratch=[pltpu.VMEM((tokens, channels), BF16), pltpu.VMEM((tokens, channels), F32)],
    )
    back = lax.all_to_all(
        done.reshape(peers, picks, tile_rows, channels), ("row", "xl"), 0, 0, tiled=True
    )
    return call(unpack_kernel, "unpack", pair_state.shape, back)


def solution(mesh):
    crops, rows, cols = (mesh.shape[name] for name in ("crop", "row", "col"))
    split = Mesh(
        mesh.devices.reshape(crops, rows, cols // 2, 2), ("crop", "row", "xl", "core")
    )
    return jax.shard_map(
        local,
        mesh=split,
        in_specs=(P(("crop", "row"), ("xl", "core"), None), P("crop")) + (P(),) * 8,
        out_specs=P(("crop", "row"), ("xl", "core"), None),
        check_vma=False,
    )
```

```python
import jax
import jax.numpy as jnp
from jax import lax
from jax.experimental import pallas as pl
from jax.experimental.pallas import tpu as pltpu
from jax.sharding import Mesh
from jax.sharding import PartitionSpec as P

F32 = jnp.float32
BF16 = jnp.bfloat16
MASKED_SCORE = -1000000000.0
CONTRACT_LAST = (((1,), (1,)), ((), ()))


def normalize(floats):
    average = jnp.mean(floats, axis=-1, keepdims=True)
    centered = floats - average
    variance = jnp.mean(centered * centered, axis=-1, keepdims=True)
    return (centered * lax.rsqrt(variance + 1e-05)).astype(BF16)


def pack_kernel(x_ref, wb_ref, out_ref):
    rows = x_ref.shape[0]
    peers, slots = out_ref.shape[:2]
    heads = wb_ref.shape[0]
    picks = slots - heads
    bias = []
    for r in range(rows):
        normed = normalize(x_ref[r].astype(F32))
        bias.append(
            lax.dot_general(wb_ref[...], normed, CONTRACT_LAST, preferred_element_type=F32)
        )
    bias = jnp.stack(bias, axis=1).astype(BF16)
    for d in range(peers):
        out_ref[d, picks:] = bias
    turned = jnp.swapaxes(x_ref[...], 0, 1)
    for q in range(picks):
        out_ref[:, q] = turned[q * peers : (q + 1) * peers]


def bias_kernel(info_ref, got_ref, out_ref):
    rows, _, heads, tile_rows, width = got_ref.shape
    tokens = rows * tile_rows
    valid = info_ref[2]
    key_ok = lax.broadcasted_iota(jnp.int32, (1, tokens), 1) < valid
    for h in range(heads):
        block = got_ref[:, 0, h].reshape(tokens, width).astype(F32)
        out_ref[h, 0] = jnp.where(key_ok, jnp.transpose(block), MASKED_SCORE).astype(BF16)


def attend_kernel(
    info_ref, x_ref, own_ref, other_ref, wq_ref, wk_ref, wv_ref, wg_ref, bg_ref, wo_ref, bo_ref,
    out_ref, bias_s,
):
    core, peer, valid = info_ref[0], info_ref[1], info_ref[2]
    rows, _, picks, tile_rows, channels = x_ref.shape
    tokens = rows * tile_rows
    heads, halves, width = own_ref.shape[:3]
    head_size = channels // heads
    tile = 128
    group = pl.program_id(0)

    @pl.when(group == 0)
    def _():
        for h in range(heads):
            for half in range(halves):
                for c, part in ((core, own_ref), (1 - core, other_ref)):
                    at = pl.multiple_of((half * 2 + c) * width, width)
                    bias_s[h, pl.ds(at, width)] = part[h, half].astype(F32)
        bias_s[heads] = jnp.zeros(bias_s.shape[1:], F32)

    weights_in = jnp.concatenate([wq_ref[...], wk_ref[...], wv_ref[...], wg_ref[...]], axis=1)
    mine = jnp.concatenate(
        [x_ref[:, 0, q].reshape(tokens, channels) for q in range(picks)], axis=0
    ).astype(F32)
    projected = jnp.dot(normalize(mine), weights_in, preferred_element_type=F32)
    gates = jax.nn.sigmoid(projected[:, 3 * channels :] + bg_ref[...])
    lane_head = lax.broadcasted_iota(jnp.int32, (1, channels), 1) // head_size
    columns = []
    for q in range(picks):
        column_ok = (group * 2 + core) * width + q * (width // picks) + peer < valid
        scale = jnp.where(column_ok, F32(head_size ** (-0.5)), F32(0.0))
        part = projected[q * tokens : (q + 1) * tokens]
        queries = (part[:, :channels] * scale).astype(BF16)
        keys = part[:, channels : 2 * channels].astype(BF16)
        values = part[:, 2 * channels : 3 * channels].astype(BF16)
        columns.append(
            (column_ok, queries, keys, jnp.concatenate([values, jnp.ones_like(values)], axis=1))
        )
    attended = [[] for _ in range(picks)]
    for at in range(0, tokens, tile):
        for q, (column_ok, queries, keys, values_ones) in enumerate(columns):
            some = queries[at : at + tile]
            stacked = jnp.concatenate(
                [jnp.where(lane_head == h, some, jnp.zeros_like(some)) for h in range(heads)],
                axis=0,
            )
            bias = jnp.concatenate(
                [bias_s[jnp.where(column_ok, h, heads), at : at + tile] for h in range(heads)],
                axis=0,
            )
            scores = lax.dot_general(stacked, keys, CONTRACT_LAST, preferred_element_type=F32)
            scores = scores + bias
            weights = jnp.exp(scores - jnp.max(scores, axis=1, keepdims=True)).astype(BF16)
            both = jnp.dot(weights, values_ones, preferred_element_type=F32)
            top = total = None
            for h in range(heads):
                one = both[h * tile : (h + 1) * tile]
                if h == 0:
                    top, total = one[:, :channels], one[:, channels:]
                else:
                    top = jnp.where(lane_head == h, one[:, :channels], top)
                    total = jnp.where(lane_head == h, one[:, channels:], total)
            attended[q].append(top / total)
    attended = jnp.concatenate([part for parts in attended for part in parts], axis=0)
    update = jnp.dot((gates * attended).astype(BF16), wo_ref[...], preferred_element_type=F32)
    out = (mine + (update + bo_ref[...])).astype(BF16)
    for q in range(picks):
        out_ref[:, 0, q] = out[q * tokens : (q + 1) * tokens].reshape(rows, tile_rows, channels)


def unpack_kernel(got_ref, out_ref):
    peers, picks = got_ref.shape[:2]
    for q in range(picks):
        out_ref[:, q * peers : (q + 1) * peers] = jnp.swapaxes(got_ref[:, q], 0, 1)


def call(kernel, name, out, *operands, grid=None, in_specs=None, out_specs=None, scratch=(), vmem=48):
    whole = pl.BlockSpec(memory_space=pltpu.VMEM)
    extra = {} if grid is None else {"grid": grid}
    return pl.pallas_call(
        kernel,
        out_shape=jax.ShapeDtypeStruct(out, BF16),
        in_specs=in_specs or [whole] * len(operands),
        out_specs=out_specs or whole,
        scratch_shapes=list(scratch),
        compiler_params=pltpu.CompilerParams(vmem_limit_bytes=vmem << 20),
        name=name,
        **extra,
    )(*operands)


def local(pair_state, valid_tokens, w_query, w_key, w_value, w_gate, b_gate, w_bias, w_out, b_out):
    tile_rows, tile_cols, channels = pair_state.shape
    heads = w_bias.shape[1]
    rows, pairs = lax.axis_size("row"), lax.axis_size("xl")
    peers = rows * pairs
    picks = tile_cols // peers
    tokens = rows * tile_rows
    core = lax.axis_index("core")
    peer = lax.axis_index("row") * pairs + lax.axis_index("xl")
    info = jnp.stack([core, peer, valid_tokens[0]]).astype(jnp.int32)
    smem = pl.BlockSpec(memory_space=pltpu.SMEM)

    part = tile_rows // 2
    sent = call(
        pack_kernel, "pack", (peers, picks + heads, tile_rows, channels), pair_state, w_bias.T,
        grid=(2,),
        in_specs=[
            pl.BlockSpec((part, tile_cols, channels), lambda a: (a, 0, 0)),
            pl.BlockSpec((heads, channels), lambda a: (0, 0)),
        ],
        out_specs=pl.BlockSpec((peers, picks + heads, part, channels), lambda a: (0, 0, a, 0)),
        vmem=62,
    )
    got = lax.all_to_all(sent, ("row", "xl"), 0, 0, tiled=True)
    got = got.reshape(rows, pairs, picks + heads, tile_rows, channels)
    own = call(
        bias_kernel, "turn_bias", (heads, pairs, tile_cols, tokens), info, got,
        grid=(pairs,),
        in_specs=[
            smem,
            pl.BlockSpec((rows, 1, heads, tile_rows, channels), lambda a: (0, a, 1, 0, 0)),
        ],
        out_specs=pl.BlockSpec((heads, 1, tile_cols, tokens), lambda a: (0, a, 0, 0)),
    )
    other = lax.ppermute(own, "core", [(0, 1), (1, 0)])
    column = pl.BlockSpec((rows, 1, picks, tile_rows, channels), lambda a: (0, a, 0, 0, 0))

    def fixed(array):
        return pl.BlockSpec(array.shape, lambda a: (0,) * array.ndim)

    operands = [own, other, w_query, w_key, w_value, w_gate, b_gate[None], w_out, b_out[None]]
    done = call(
        attend_kernel, "attend", (rows, pairs, picks, tile_rows, channels), info, got, *operands,
        grid=(pairs,),
        in_specs=[smem, column] + [fixed(array) for array in operands],
        out_specs=column,
        scratch=[pltpu.VMEM((heads + 1, tokens, tokens), F32)],
    )
    back = lax.all_to_all(
        done.reshape(peers, picks, tile_rows, channels), ("row", "xl"), 0, 0, tiled=True
    )
    return call(unpack_kernel, "unpack", pair_state.shape, back)


def solution(mesh):
    crops, rows, cols = (mesh.shape[name] for name in ("crop", "row", "col"))
    split = Mesh(
        mesh.devices.reshape(crops, rows, cols // 2, 2), ("crop", "row", "xl", "core")
    )
    return jax.shard_map(
        local,
        mesh=split,
        in_specs=(P(("crop", "row"), ("xl", "core"), None), P("crop")) + (P(),) * 8,
        out_specs=P(("crop", "row"), ("xl", "core"), None),
        check_vma=False,
    )
```

```python
import functools

import jax
import jax.numpy as jnp
from jax import lax
from jax.experimental import pallas as pl
from jax.experimental.pallas import tpu as pltpu
from jax.sharding import Mesh
from jax.sharding import PartitionSpec as P

F32 = jnp.float32
BF16 = jnp.bfloat16
MASKED_SCORE = -1000000000.0
CONTRACT_LAST = (((1,), (1,)), ((), ()))
MICROSECOND = 1_150_000_000
WHOLE = pl.BlockSpec(memory_space=pltpu.VMEM)
SCALARS = pl.BlockSpec(memory_space=pltpu.SMEM)


def normalize(floats):
    average = jnp.mean(floats, axis=-1, keepdims=True)
    centered = floats - average
    variance = jnp.mean(centered * centered, axis=-1, keepdims=True)
    return (centered * lax.rsqrt(variance + 1e-05)).astype(BF16)


def pack_kernel(x_ref, wb_ref, out_ref):
    rows = x_ref.shape[0]
    peers, slots = out_ref.shape[:2]
    heads = wb_ref.shape[0]
    picks = slots - heads
    bias = []
    for r in range(rows):
        normed = normalize(x_ref[r].astype(F32))
        bias.append(
            lax.dot_general(wb_ref[...], normed, CONTRACT_LAST, preferred_element_type=F32)
        )
    bias = jnp.stack(bias, axis=1).astype(BF16)
    for d in range(peers):
        out_ref[d, picks:] = bias
    turned = jnp.swapaxes(x_ref[...], 0, 1)
    for q in range(picks):
        out_ref[:, q] = turned[q * peers : (q + 1) * peers]


def bias_kernel(info_ref, got_ref, out_ref):
    heads, width, tokens = out_ref.shape
    first = got_ref.shape[1] - heads
    key_ok = lax.broadcasted_iota(jnp.int32, (1, tokens), 1) < info_ref[3]
    for h in range(heads):
        block = got_ref[:, first + h].reshape(tokens, width).astype(F32)
        out_ref[h] = jnp.where(key_ok, jnp.transpose(block), MASKED_SCORE).astype(BF16)


def column_is_real(info_ref, q, peers, width):
    column = (info_ref[1] * 2 + info_ref[0]) * width + q * peers + info_ref[2]
    return column < info_ref[3]


def project_kernel(
    info_ref, got_ref, wq_ref, wk_ref, wv_ref, wg_ref, bg_ref, qkv_ref, gate_ref, *, head_size
):
    rows, _, tile_rows, channels = got_ref.shape
    picks, tokens = qkv_ref.shape[:2]
    group = picks // 2
    weights_in = jnp.concatenate([wq_ref[...], wk_ref[...], wv_ref[...], wg_ref[...]], axis=1)
    for first in range(0, picks, group):
        mine = jnp.concatenate(
            [got_ref[:, first + q].reshape(tokens, channels) for q in range(group)], axis=0
        ).astype(F32)
        projected = jnp.dot(normalize(mine), weights_in, preferred_element_type=F32)
        for q in range(group):
            real = column_is_real(info_ref, first + q, rows, rows * picks)
            scale = jnp.where(real, F32(head_size ** (-0.5)), F32(0.0))
            queries = projected[q * tokens : (q + 1) * tokens, :channels] * scale
            qkv_ref[first + q, :, :channels] = queries.astype(BF16)
        some = pl.ds(first, group)
        qkv_ref[some, :, channels:] = (
            projected[:, channels : 3 * channels].astype(BF16).reshape(group, tokens, -1)
        )
        gate_ref[some] = jax.nn.sigmoid(projected[:, 3 * channels :] + bg_ref[...]).reshape(
            group, tokens, channels
        )


def attend_kernel(info_ref, got_ref, qkv_ref, gate_ref, wo_ref, bo_ref, *refs, far):
    blocks, out_ref, bias_s = refs[:-2], refs[-2], refs[-1]
    core, pair = info_ref[0], info_ref[1]
    rows, _, tile_rows, channels = got_ref.shape
    picks, tokens = qkv_ref.shape[:2]
    heads, width = blocks[0].shape[:2]
    head_size = channels // heads
    tiles = width // tile_rows
    half = 1 - pair if far else pair
    bias_s[heads] = jnp.zeros(bias_s.shape[1:], F32)
    starts = []
    for n, block in enumerate(blocks):
        for h in range(heads):
            bias_s[h, n * width : (n + 1) * width] = block[h].astype(F32)
        mine = core if (n == 0) == (far != 2) else 1 - core
        starts.append((half * 2 + mine) * width)
    lane_head = lax.broadcasted_iota(jnp.int32, (1, channels), 1) // head_size
    for n, start in enumerate(starts):
        at = pl.ds(pl.multiple_of(start, width), width)
        attended = []
        for q in range(picks):
            real = column_is_real(info_ref, q, rows, width)
            some = qkv_ref[q, at, :channels]
            keys = qkv_ref[q, :, channels : 2 * channels]
            values = qkv_ref[q, :, 2 * channels :]
            values_ones = jnp.concatenate([values, jnp.ones_like(values)], axis=1)
            stacked = jnp.concatenate(
                [jnp.where(lane_head == h, some, jnp.zeros_like(some)) for h in range(heads)],
                axis=0,
            )
            bias = jnp.concatenate(
                [
                    bias_s[jnp.where(real, h, heads), n * width : (n + 1) * width]
                    for h in range(heads)
                ],
                axis=0,
            )
            scores = lax.dot_general(stacked, keys, CONTRACT_LAST, preferred_element_type=F32)
            scores = scores + bias
            weights = jnp.exp(scores - jnp.max(scores, axis=1, keepdims=True)).astype(BF16)
            both = jnp.dot(weights, values_ones, preferred_element_type=F32)
            top = total = None
            for h in range(heads):
                one = both[h * width : (h + 1) * width]
                if h == 0:
                    top, total = one[:, :channels], one[:, channels:]
                else:
                    top = jnp.where(lane_head == h, one[:, :channels], top)
                    total = jnp.where(lane_head == h, one[:, channels:], total)
            attended.append(gate_ref[q, at] * (top / total))
        mix = jnp.concatenate(attended, axis=0).astype(BF16)
        update = jnp.dot(mix, wo_ref[...], preferred_element_type=F32) + bo_ref[...]
        tile = pl.ds(start // tile_rows, tiles)
        for q in range(picks):
            state = got_ref[tile, q].reshape(width, channels).astype(F32)
            out = (state + update[q * width : (q + 1) * width]).astype(BF16)
            out_ref[n * tiles : (n + 1) * tiles, q] = out.reshape(tiles, tile_rows, channels)


def gather_kernel(info_ref, near_ref, far_ref, last_ref, out_ref):
    core, pair = info_ref[0], info_ref[1]
    tiles = far_ref.shape[0]
    for part, first, half, mine in (
        (near_ref, 0, pair, core),
        (near_ref, tiles, pair, 1 - core),
        (far_ref, 0, 1 - pair, core),
        (last_ref, 0, 1 - pair, 1 - core),
    ):
        out_ref[pl.ds((half * 2 + mine) * tiles, tiles)] = part[first : first + tiles]


def unpack_kernel(got_ref, out_ref):
    peers, picks = got_ref.shape[:2]
    for q in range(picks):
        out_ref[:, q * peers : (q + 1) * peers] = jnp.swapaxes(got_ref[:, q], 0, 1)


def call(kernel, name, out, *operands, cost, vmem=28, scratch=(), **grid):
    grid.setdefault("in_specs", [SCALARS if o.ndim == 1 else WHOLE for o in operands])
    grid.setdefault("out_specs", jax.tree.map(lambda _: WHOLE, out))
    return pl.pallas_call(
        kernel,
        out_shape=out,
        scratch_shapes=list(scratch),
        compiler_params=pltpu.CompilerParams(vmem_limit_bytes=vmem << 20),
        cost_estimate=pl.CostEstimate(flops=cost, bytes_accessed=0, transcendentals=0),
        name=name,
        **grid,
    )(*operands)


def local(pair_state, valid_tokens, w_query, w_key, w_value, w_gate, b_gate, w_bias, w_out, b_out):
    tile_rows, tile_cols, channels = pair_state.shape
    heads = w_bias.shape[1]
    peers = lax.axis_size("row")
    picks = tile_cols // peers
    tokens = peers * tile_rows
    info = jnp.stack(
        [lax.axis_index("core"), lax.axis_index("xl"), lax.axis_index("row"), valid_tokens[0]]
    ).astype(jnp.int32)
    of = jax.ShapeDtypeStruct
    swap = [(0, 1), (1, 0)]

    part = tile_rows // 2
    slots = picks + heads
    sent = call(
        pack_kernel, "pack", of((peers, slots, tile_rows, channels), BF16), pair_state, w_bias.T,
        grid=(2,),
        in_specs=[
            pl.BlockSpec((part, tile_cols, channels), lambda a: (a, 0, 0)),
            pl.BlockSpec((heads, channels), lambda a: (0, 0)),
        ],
        out_specs=pl.BlockSpec((peers, slots, part, channels), lambda a: (0, 0, a, 0)),
        cost=4 * MICROSECOND, vmem=62,
    )
    got = lax.all_to_all(sent, "row", 0, 0, tiled=True)
    own = call(bias_kernel, "turn_bias", of((heads, tile_cols, tokens), BF16), info, got, cost=MICROSECOND)
    far = lax.ppermute(own, "xl", swap)
    near = lax.ppermute(own, "core", swap)
    qkv, gate = call(
        functools.partial(project_kernel, head_size=channels // heads), "project",
        (of((picks, tokens, 3 * channels), BF16), of((picks, tokens, channels), F32)),
        info, got, w_query, w_key, w_value, w_gate, b_gate[None],
        cost=3 * MICROSECOND,
    )

    def attend(name, far, *blocks):
        count = len(blocks)
        return call(
            functools.partial(attend_kernel, far=far), name,
            of((count * tile_cols // tile_rows, picks, tile_rows, channels), BF16),
            info, got, qkv, gate, w_out, b_out[None], *blocks,
            cost=3 * count * MICROSECOND,
            scratch=[pltpu.VMEM((heads + 1, count * tile_cols, tokens), F32)],
        )

    first = attend("attend_near", 0, own, near)
    far, first = lax.optimization_barrier((far, first))
    last = lax.ppermute(far, "core", swap)
    second = attend("attend_far", 1, far)
    done = [first, second, attend("attend_last", 2, last)]
    done = call(
        gather_kernel, "order", of((peers, picks, tile_rows, channels), BF16), info, *done,
        cost=MICROSECOND,
    )
    back = lax.all_to_all(done, "row", 0, 0, tiled=True)
    return call(unpack_kernel, "unpack", of(pair_state.shape, BF16), back, cost=MICROSECOND)


def solution(mesh):
    crops, rows, cols = (mesh.shape[name] for name in ("crop", "row", "col"))
    split = Mesh(
        mesh.devices.reshape(crops, rows, cols // 2, 2), ("crop", "row", "xl", "core")
    )
    return jax.shard_map(
        local,
        mesh=split,
        in_specs=(P(("crop", "row"), ("xl", "core"), None), P("crop")) + (P(),) * 8,
        out_specs=P(("crop", "row"), ("xl", "core"), None),
        check_vma=False,
    )
```

```python
import functools

import jax
import jax.numpy as jnp
from jax import lax
from jax.experimental import pallas as pl
from jax.experimental.pallas import tpu as pltpu
from jax.sharding import Mesh
from jax.sharding import PartitionSpec as P

F32 = jnp.float32
BF16 = jnp.bfloat16
MASKED_SCORE = -1000000000.0
CONTRACT_LAST = (((1,), (1,)), ((), ()))
MICROSECOND = 1_150_000_000
ORDER = (10, 14, 5, 1, 9, 2, 3, 11, 13, 7, 8, 4, 0, 6, 15, 12)
PLACE = tuple(ORDER.index(row) for row in range(len(ORDER)))
WHOLE = pl.BlockSpec(memory_space=pltpu.VMEM)
SCALARS = pl.BlockSpec(memory_space=pltpu.SMEM)


def normalize(floats):
    average = jnp.mean(floats, axis=-1, keepdims=True)
    centered = floats - average
    variance = jnp.mean(centered * centered, axis=-1, keepdims=True)
    return (centered * lax.rsqrt(variance + 1e-05)).astype(BF16)


def pack_kernel(x_ref, wb_ref, out_ref):
    rows = x_ref.shape[0]
    peers, slots = out_ref.shape[:2]
    heads = wb_ref.shape[0]
    picks = slots - heads
    bias = []
    for r in range(rows):
        normed = normalize(x_ref[r].astype(F32))
        bias.append(
            lax.dot_general(wb_ref[...], normed, CONTRACT_LAST, preferred_element_type=F32)
        )
    bias = jnp.stack(bias, axis=1).astype(BF16)
    for d in range(peers):
        out_ref[d, picks:] = bias
    turned = jnp.swapaxes(x_ref[...], 0, 1)
    for q in range(picks):
        out_ref[:, q] = turned[q * peers : (q + 1) * peers]


def bias_kernel(info_ref, got_ref, out_ref):
    heads, width, tokens = out_ref.shape
    first = got_ref.shape[1] - heads
    key_ok = lax.broadcasted_iota(jnp.int32, (1, tokens), 1) < info_ref[3]
    for h in range(heads):
        block = jnp.concatenate([got_ref[at, first + h] for at in PLACE], axis=0).astype(F32)
        out_ref[h] = jnp.where(key_ok, jnp.transpose(block), MASKED_SCORE).astype(BF16)


def column_is_real(info_ref, q, peers, width):
    column = (info_ref[1] * 2 + info_ref[0]) * width + q * peers + info_ref[2]
    return column < info_ref[3]


def project_kernel(
    info_ref, got_ref, wq_ref, wk_ref, wv_ref, wg_ref, bg_ref, qkv_ref, gate_ref, *, head_size
):
    rows, _, tile_rows, channels = got_ref.shape
    picks, tokens = qkv_ref.shape[:2]
    group = picks // 2
    weights_in = jnp.concatenate([wq_ref[...], wk_ref[...], wv_ref[...], wg_ref[...]], axis=1)
    for first in range(0, picks, group):
        mine = jnp.concatenate(
            [got_ref[at, first + q] for q in range(group) for at in PLACE], axis=0
        ).astype(F32)
        projected = jnp.dot(normalize(mine), weights_in, preferred_element_type=F32)
        for q in range(group):
            real = column_is_real(info_ref, first + q, rows, rows * picks)
            scale = jnp.where(real, F32(head_size ** (-0.5)), F32(0.0))
            part = projected[q * tokens : (q + 1) * tokens]
            qkv_ref[first + q, :, :channels] = (part[:, :channels] * scale).astype(BF16)
            qkv_ref[first + q, :, channels:] = part[:, channels : 3 * channels].astype(BF16)
            gate_ref[first + q] = jax.nn.sigmoid(part[:, 3 * channels :] + bg_ref[...])


def attend_kernel(info_ref, got_ref, qkv_ref, gate_ref, wo_ref, bo_ref, *refs, far):
    blocks, out_ref, bias_s = refs[:-2], refs[-2], refs[-1]
    core, pair = info_ref[0], info_ref[1]
    earlier, blocks = (blocks[:2], blocks[2:]) if far == 2 else ((), blocks)
    rows, _, tile_rows, channels = got_ref.shape
    picks, tokens = qkv_ref.shape[:2]
    heads, width = blocks[0].shape[:2]
    head_size = channels // heads
    tiles = width // tile_rows
    half = 1 - pair if far else pair
    bias_s[heads] = jnp.zeros(bias_s.shape[1:], F32)
    starts = []
    for n, block in enumerate(blocks):
        for h in range(heads):
            bias_s[h, n * width : (n + 1) * width] = block[h].astype(F32)
        mine = core if (n == 0) == (far != 2) else 1 - core
        starts.append((half * 2 + mine) * width)
    lane_head = lax.broadcasted_iota(jnp.int32, (1, channels), 1) // head_size
    for n, start in enumerate(starts):
        at = pl.ds(pl.multiple_of(start, width), width)
        attended = []
        for q in range(picks):
            real = column_is_real(info_ref, q, rows, width)
            some = qkv_ref[q, at, :channels]
            keys = qkv_ref[q, :, channels : 2 * channels]
            values = qkv_ref[q, :, 2 * channels :]
            values_ones = jnp.concatenate([values, jnp.ones_like(values)], axis=1)
            stacked = jnp.concatenate(
                [jnp.where(lane_head == h, some, jnp.zeros_like(some)) for h in range(heads)],
                axis=0,
            )
            bias = jnp.concatenate(
                [
                    bias_s[jnp.where(real, h, heads), n * width : (n + 1) * width]
                    for h in range(heads)
                ],
                axis=0,
            )
            scores = lax.dot_general(stacked, keys, CONTRACT_LAST, preferred_element_type=F32)
            scores = scores + bias
            weights = jnp.exp(scores - jnp.max(scores, axis=1, keepdims=True)).astype(BF16)
            both = jnp.dot(weights, values_ones, preferred_element_type=F32)
            top = total = None
            for h in range(heads):
                one = both[h * width : (h + 1) * width]
                if h == 0:
                    top, total = one[:, :channels], one[:, channels:]
                else:
                    top = jnp.where(lane_head == h, one[:, :channels], top)
                    total = jnp.where(lane_head == h, one[:, channels:], total)
            attended.append(gate_ref[q, at] * (top / total))
        mix = jnp.concatenate(attended, axis=0).astype(BF16)
        update = jnp.dot(mix, wo_ref[...], preferred_element_type=F32) + bo_ref[...]
        for t in range(tiles):
            place = info_ref[4 + start // tile_rows + t]
            to = place if earlier else n * tiles + t
            for q in range(picks):
                change = update[q * width + t * tile_rows : q * width + (t + 1) * tile_rows]
                out_ref[to, q] = (got_ref[place, q].astype(F32) + change).astype(BF16)
    if earlier:
        near_ref, far_ref = earlier
        for part, first, half_of, mine in (
            (near_ref, 0, pair, core),
            (near_ref, tiles, pair, 1 - core),
            (far_ref, 0, half, core),
        ):
            for t in range(tiles):
                to = info_ref[4 + (half_of * 2 + mine) * tiles + t]
                out_ref[to] = part[first + t]


def unpack_kernel(got_ref, out_ref):
    peers, picks = got_ref.shape[:2]
    for q in range(picks):
        out_ref[:, q * peers : (q + 1) * peers] = jnp.swapaxes(got_ref[:, q], 0, 1)


def call(kernel, name, out, *operands, cost, vmem=28, scratch=(), **grid):
    grid.setdefault("in_specs", [SCALARS if o.ndim == 1 else WHOLE for o in operands])
    grid.setdefault("out_specs", jax.tree.map(lambda _: WHOLE, out))
    return pl.pallas_call(
        kernel,
        out_shape=out,
        scratch_shapes=list(scratch),
        compiler_params=pltpu.CompilerParams(vmem_limit_bytes=vmem << 20),
        cost_estimate=pl.CostEstimate(flops=cost, bytes_accessed=0, transcendentals=0),
        name=name,
        **grid,
    )(*operands)


def local(pair_state, valid_tokens, w_query, w_key, w_value, w_gate, b_gate, w_bias, w_out, b_out):
    tile_rows, tile_cols, channels = pair_state.shape
    heads = w_bias.shape[1]
    peers = lax.axis_size("row")
    picks = tile_cols // peers
    tokens = peers * tile_rows
    place = jnp.array(PLACE, jnp.int32)
    here = [lax.axis_index("core"), lax.axis_index("xl"), place[lax.axis_index("row")]]
    info = jnp.concatenate([jnp.stack(here + [valid_tokens[0]]).astype(jnp.int32), place])
    of = jax.ShapeDtypeStruct
    swap = [(0, 1), (1, 0)]

    def exchange(array):
        return lax.all_to_all(array, "row", 0, 0, axis_index_groups=[list(ORDER)], tiled=True)

    part = tile_rows // 2
    slots = picks + heads
    sent = call(
        pack_kernel, "pack", of((peers, slots, tile_rows, channels), BF16), pair_state, w_bias.T,
        grid=(2,),
        in_specs=[
            pl.BlockSpec((part, tile_cols, channels), lambda a: (a, 0, 0)),
            pl.BlockSpec((heads, channels), lambda a: (0, 0)),
        ],
        out_specs=pl.BlockSpec((peers, slots, part, channels), lambda a: (0, 0, a, 0)),
        cost=4 * MICROSECOND, vmem=62,
    )
    got = exchange(sent)
    own = call(bias_kernel, "turn_bias", of((heads, tile_cols, tokens), BF16), info, got, cost=MICROSECOND)
    far = lax.ppermute(own, "xl", swap)
    near = lax.ppermute(own, "core", swap)
    qkv, gate = call(
        functools.partial(project_kernel, head_size=channels // heads), "project",
        (of((picks, tokens, 3 * channels), BF16), of((picks, tokens, channels), F32)),
        info, got, w_query, w_key, w_value, w_gate, b_gate[None],
        cost=3 * MICROSECOND,
    )

    def attend(name, far, *blocks, earlier=()):
        count = len(blocks)
        tiles = peers if earlier else count * tile_cols // tile_rows
        return call(
            functools.partial(attend_kernel, far=far), name,
            of((tiles, picks, tile_rows, channels), BF16),
            info, got, qkv, gate, w_out, b_out[None], *earlier, *blocks,
            cost=3 * count * MICROSECOND,
            scratch=[pltpu.VMEM((heads + 1, count * tile_cols, tokens), F32)],
        )

    first = attend("attend_near", 0, own, near)
    far, first = lax.optimization_barrier((far, first))
    last = lax.ppermute(far, "core", swap)
    second = attend("attend_far", 1, far)
    done = attend("attend_last", 2, last, earlier=(first, second))
    back = exchange(done)
    return call(unpack_kernel, "unpack", of(pair_state.shape, BF16), back, cost=MICROSECOND)


def solution(mesh):
    crops, rows, cols = (mesh.shape[name] for name in ("crop", "row", "col"))
    split = Mesh(
        mesh.devices.reshape(crops, rows, cols // 2, 2), ("crop", "row", "xl", "core")
    )
    return jax.shard_map(
        local,
        mesh=split,
        in_specs=(P(("crop", "row"), ("xl", "core"), None), P("crop")) + (P(),) * 8,
        out_specs=P(("crop", "row"), ("xl", "core"), None),
        check_vma=False,
    )
```

```python
import functools

import jax
import jax.numpy as jnp
from jax import lax
from jax.experimental import pallas as pl
from jax.experimental.pallas import tpu as pltpu
from jax.sharding import Mesh
from jax.sharding import PartitionSpec as P

F32 = jnp.float32
BF16 = jnp.bfloat16
MASKED_SCORE = -1000000000.0
CONTRACT_LAST = (((1,), (1,)), ((), ()))
MICROSECOND = 1_150_000_000
ORDER = (10, 5, 0, 1, 9, 4, 6, 2, 3, 15, 11, 7, 12, 8, 13, 14)
ORDER_BACK = (10, 14, 5, 1, 9, 2, 3, 11, 13, 7, 8, 4, 0, 6, 15, 12)
PLACE = tuple(ORDER.index(row) for row in range(len(ORDER)))
PLACE_BACK = tuple(ORDER_BACK.index(row) for row in range(len(ORDER)))
WHOLE = pl.BlockSpec(memory_space=pltpu.VMEM)
SCALARS = pl.BlockSpec(memory_space=pltpu.SMEM)


def normalize(floats):
    average = jnp.mean(floats, axis=-1, keepdims=True)
    centered = floats - average
    variance = jnp.mean(centered * centered, axis=-1, keepdims=True)
    return (centered * lax.rsqrt(variance + 1e-05)).astype(BF16)


def pack_kernel(x_ref, wb_ref, out_ref):
    rows = x_ref.shape[0]
    peers, slots = out_ref.shape[:2]
    heads = wb_ref.shape[0]
    picks = slots - heads
    cols = x_ref.shape[1]
    normed = normalize(x_ref[...].reshape(rows * cols, -1).astype(F32))
    bias = lax.dot_general(wb_ref[...], normed, CONTRACT_LAST, preferred_element_type=F32)
    bias = jnp.stack([bias[:, r * cols : (r + 1) * cols] for r in range(rows)], axis=1)
    bias = bias.astype(BF16)
    for d in range(peers):
        out_ref[d, picks:] = bias
    turned = jnp.swapaxes(x_ref[...], 0, 1)
    for q in range(picks):
        out_ref[:, q] = turned[q * peers : (q + 1) * peers]


def bias_kernel(info_ref, got_ref, out_ref):
    heads, width, tokens = out_ref.shape
    first = got_ref.shape[1] - heads
    key_ok = lax.broadcasted_iota(jnp.int32, (1, tokens), 1) < info_ref[3]
    for h in range(heads):
        block = jnp.concatenate([got_ref[at, first + h] for at in PLACE], axis=0).astype(F32)
        out_ref[h] = jnp.where(key_ok, jnp.transpose(block), MASKED_SCORE).astype(BF16)


def column_is_real(info_ref, q, peers, width):
    column = (info_ref[1] * 2 + info_ref[0]) * width + q * peers + info_ref[2]
    return column < info_ref[3]


def project_kernel(
    info_ref, got_ref, wq_ref, wk_ref, wv_ref, wg_ref, bg_ref, qkv_ref, gate_ref, *, head_size
):
    rows, _, tile_rows, channels = got_ref.shape
    picks, tokens = qkv_ref.shape[:2]
    group = picks // 2
    weights_in = jnp.concatenate([wq_ref[...], wk_ref[...], wv_ref[...], wg_ref[...]], axis=1)
    for first in range(0, picks, group):
        mine = jnp.concatenate(
            [got_ref[at, first + q] for q in range(group) for at in PLACE], axis=0
        ).astype(F32)
        projected = jnp.dot(normalize(mine), weights_in, preferred_element_type=F32)
        for q in range(group):
            real = column_is_real(info_ref, first + q, rows, rows * picks)
            scale = jnp.where(real, F32(head_size ** (-0.5)), F32(0.0))
            part = projected[q * tokens : (q + 1) * tokens]
            qkv_ref[first + q, :, :channels] = (part[:, :channels] * scale).astype(BF16)
            qkv_ref[first + q, :, channels:] = part[:, channels : 3 * channels].astype(BF16)
            gate_ref[first + q] = jax.nn.sigmoid(part[:, 3 * channels :] + bg_ref[...])


def attend_kernel(info_ref, got_ref, qkv_ref, gate_ref, wo_ref, bo_ref, *refs, far):
    blocks, out_ref, bias_s = refs[:-2], refs[-2], refs[-1]
    core, pair = info_ref[0], info_ref[1]
    earlier, blocks = (blocks[:2], blocks[2:]) if far == 2 else ((), blocks)
    rows, _, tile_rows, channels = got_ref.shape
    picks, tokens = qkv_ref.shape[:2]
    heads, width = blocks[0].shape[:2]
    head_size = channels // heads
    tiles = width // tile_rows
    half = 1 - pair if far else pair
    bias_s[heads] = jnp.zeros(bias_s.shape[1:], F32)
    starts = []
    for n, block in enumerate(blocks):
        for h in range(heads):
            bias_s[h, n * width : (n + 1) * width] = block[h].astype(F32)
        mine = core if (n == 0) == (far != 2) else 1 - core
        starts.append((half * 2 + mine) * width)
    lane_head = lax.broadcasted_iota(jnp.int32, (1, channels), 1) // head_size
    for n, start in enumerate(starts):
        at = pl.ds(pl.multiple_of(start, width), width)
        attended = []
        for q in range(picks):
            real = column_is_real(info_ref, q, rows, width)
            some = qkv_ref[q, at, :channels]
            keys = qkv_ref[q, :, channels : 2 * channels]
            values = qkv_ref[q, :, 2 * channels :]
            values_ones = jnp.concatenate([values, jnp.ones_like(values)], axis=1)
            stacked = jnp.concatenate(
                [jnp.where(lane_head == h, some, jnp.zeros_like(some)) for h in range(heads)],
                axis=0,
            )
            bias = jnp.concatenate(
                [
                    bias_s[jnp.where(real, h, heads), n * width : (n + 1) * width]
                    for h in range(heads)
                ],
                axis=0,
            )
            scores = lax.dot_general(stacked, keys, CONTRACT_LAST, preferred_element_type=F32)
            scores = scores + bias
            weights = jnp.exp(scores - jnp.max(scores, axis=1, keepdims=True)).astype(BF16)
            both = jnp.dot(weights, values_ones, preferred_element_type=F32)
            top = total = None
            for h in range(heads):
                one = both[h * width : (h + 1) * width]
                if h == 0:
                    top, total = one[:, :channels], one[:, channels:]
                else:
                    top = jnp.where(lane_head == h, one[:, :channels], top)
                    total = jnp.where(lane_head == h, one[:, channels:], total)
            attended.append(gate_ref[q, at] * (top / total))
        mix = jnp.concatenate(attended, axis=0).astype(BF16)
        update = jnp.dot(mix, wo_ref[...], preferred_element_type=F32) + bo_ref[...]
        for t in range(tiles):
            place = info_ref[4 + start // tile_rows + t]
            to = info_ref[4 + rows + start // tile_rows + t] if earlier else n * tiles + t
            for q in range(picks):
                change = update[q * width + t * tile_rows : q * width + (t + 1) * tile_rows]
                out_ref[to, q] = (got_ref[place, q].astype(F32) + change).astype(BF16)
    if earlier:
        near_ref, far_ref = earlier
        for part, first, half_of, mine in (
            (near_ref, 0, pair, core),
            (near_ref, tiles, pair, 1 - core),
            (far_ref, 0, half, core),
        ):
            for t in range(tiles):
                to = info_ref[4 + rows + (half_of * 2 + mine) * tiles + t]
                out_ref[to] = part[first + t]


def unpack_kernel(got_ref, out_ref):
    peers, picks = got_ref.shape[:2]
    for q in range(picks):
        columns = jnp.stack([got_ref[PLACE_BACK[row], q] for row in ORDER], axis=0)
        out_ref[:, q * peers : (q + 1) * peers] = jnp.swapaxes(columns, 0, 1)


def call(kernel, name, out, *operands, cost, vmem=28, scratch=(), **grid):
    grid.setdefault("in_specs", [SCALARS if o.ndim == 1 else WHOLE for o in operands])
    grid.setdefault("out_specs", jax.tree.map(lambda _: WHOLE, out))
    return pl.pallas_call(
        kernel,
        out_shape=out,
        scratch_shapes=list(scratch),
        compiler_params=pltpu.CompilerParams(vmem_limit_bytes=vmem << 20),
        cost_estimate=pl.CostEstimate(flops=cost, bytes_accessed=0, transcendentals=0),
        name=name,
        **grid,
    )(*operands)


def local(pair_state, valid_tokens, w_query, w_key, w_value, w_gate, b_gate, w_bias, w_out, b_out):
    tile_rows, tile_cols, channels = pair_state.shape
    heads = w_bias.shape[1]
    peers = lax.axis_size("row")
    picks = tile_cols // peers
    tokens = peers * tile_rows
    places = jnp.array(PLACE + PLACE_BACK, jnp.int32)
    here = [lax.axis_index("core"), lax.axis_index("xl"), places[lax.axis_index("row")]]
    info = jnp.concatenate([jnp.stack(here + [valid_tokens[0]]).astype(jnp.int32), places])
    of = jax.ShapeDtypeStruct
    swap = [(0, 1), (1, 0)]

    def exchange(array, order):
        return lax.all_to_all(array, "row", 0, 0, axis_index_groups=[list(order)], tiled=True)

    part = tile_rows // 2
    slots = picks + heads
    sent = call(
        pack_kernel, "pack", of((peers, slots, tile_rows, channels), BF16), pair_state, w_bias.T,
        grid=(2,),
        in_specs=[
            pl.BlockSpec((part, tile_cols, channels), lambda a: (a, 0, 0)),
            pl.BlockSpec((heads, channels), lambda a: (0, 0)),
        ],
        out_specs=pl.BlockSpec((peers, slots, part, channels), lambda a: (0, 0, a, 0)),
        cost=4 * MICROSECOND, vmem=62,
    )
    got = exchange(sent, ORDER)
    own = call(bias_kernel, "turn_bias", of((heads, tile_cols, tokens), BF16), info, got, cost=MICROSECOND)
    far = lax.ppermute(own, "xl", swap)
    near = lax.ppermute(own, "core", swap)
    qkv, gate = call(
        functools.partial(project_kernel, head_size=channels // heads), "project",
        (of((picks, tokens, 3 * channels), BF16), of((picks, tokens, channels), F32)),
        info, got, w_query, w_key, w_value, w_gate, b_gate[None],
        cost=3 * MICROSECOND,
    )

    def attend(name, far, *blocks, earlier=()):
        count = len(blocks)
        tiles = peers if earlier else count * tile_cols // tile_rows
        return call(
            functools.partial(attend_kernel, far=far), name,
            of((tiles, picks, tile_rows, channels), BF16),
            info, got, qkv, gate, w_out, b_out[None], *earlier, *blocks,
            cost=3 * count * MICROSECOND,
            scratch=[pltpu.VMEM((heads + 1, count * tile_cols, tokens), F32)],
        )

    first = attend("attend_near", 0, own, near)
    far, first = lax.optimization_barrier((far, first))
    last = lax.ppermute(far, "core", swap)
    second = attend("attend_far", 1, far)
    done = attend("attend_last", 2, last, earlier=(first, second))
    back = exchange(done, ORDER_BACK)
    return call(unpack_kernel, "unpack", of(pair_state.shape, BF16), back, cost=MICROSECOND)


def solution(mesh):
    crops, rows, cols = (mesh.shape[name] for name in ("crop", "row", "col"))
    split = Mesh(
        mesh.devices.reshape(crops, rows, cols // 2, 2), ("crop", "row", "xl", "core")
    )
    return jax.shard_map(
        local,
        mesh=split,
        in_specs=(P(("crop", "row"), ("xl", "core"), None), P("crop")) + (P(),) * 8,
        out_specs=P(("crop", "row"), ("xl", "core"), None),
        check_vma=False,
    )
```

```python
import functools

import jax
import jax.numpy as jnp
from jax import lax
from jax.experimental import pallas as pl
from jax.experimental.pallas import tpu as pltpu
from jax.sharding import Mesh
from jax.sharding import PartitionSpec as P

F32 = jnp.float32
BF16 = jnp.bfloat16
MASKED_SCORE = -1000000000.0
CONTRACT_LAST = (((1,), (1,)), ((), ()))
MICROSECOND = 1_150_000_000
ORDER = (10, 5, 0, 1, 9, 4, 6, 2, 3, 15, 11, 7, 12, 8, 13, 14)
ORDER_BACK = (10, 14, 5, 1, 9, 2, 3, 11, 13, 7, 8, 4, 0, 6, 15, 12)
PLACE = tuple(ORDER.index(row) for row in range(len(ORDER)))
PLACE_BACK = tuple(ORDER_BACK.index(row) for row in range(len(ORDER)))
WHOLE = pl.BlockSpec(memory_space=pltpu.VMEM)
SCALARS = pl.BlockSpec(memory_space=pltpu.SMEM)


def normalize(floats):
    average = jnp.mean(floats, axis=-1, keepdims=True)
    centered = floats - average
    variance = jnp.mean(centered * centered, axis=-1, keepdims=True)
    return (centered * lax.rsqrt(variance + 1e-05)).astype(BF16)


def pack_kernel(x_ref, wb_ref, out_ref):
    rows = x_ref.shape[0]
    peers, slots = out_ref.shape[:2]
    heads = wb_ref.shape[0]
    picks = slots - heads
    cols = x_ref.shape[1]
    normed = normalize(x_ref[...].reshape(rows * cols, -1).astype(F32))
    bias = lax.dot_general(wb_ref[...], normed, CONTRACT_LAST, preferred_element_type=F32)
    bias = jnp.stack([bias[:, r * cols : (r + 1) * cols] for r in range(rows)], axis=1)
    bias = bias.astype(BF16)
    for d in range(peers):
        out_ref[d, picks:] = bias
    turned = jnp.swapaxes(x_ref[...], 0, 1)
    for q in range(picks):
        out_ref[:, q] = turned[q * peers : (q + 1) * peers]


def bias_kernel(info_ref, got_ref, out_ref):
    heads, width, tokens = out_ref.shape
    first = got_ref.shape[1] - heads
    key_ok = lax.broadcasted_iota(jnp.int32, (1, tokens), 1) < info_ref[3]
    for h in range(heads):
        block = jnp.concatenate([got_ref[at, first + h] for at in PLACE], axis=0).astype(F32)
        out_ref[h] = jnp.where(key_ok, jnp.transpose(block), MASKED_SCORE).astype(BF16)


def column_is_real(info_ref, q, peers, width):
    column = (info_ref[1] * 2 + info_ref[0]) * width + q * peers + info_ref[2]
    return column < info_ref[3]


def project_kernel(
    info_ref, got_ref, wq_ref, wk_ref, wv_ref, wg_ref, bg_ref, qkv_ref, gate_ref, even_ref, *,
    head_size
):
    rows, _, tile_rows, channels = got_ref.shape
    picks, tokens = qkv_ref.shape[:2]
    group = picks // 2
    weights_in = jnp.concatenate([wq_ref[...], wk_ref[...], wv_ref[...], wg_ref[...]], axis=1)
    for first in range(0, picks, group):
        mine = jnp.concatenate(
            [got_ref[at, first + q] for q in range(group) for at in PLACE], axis=0
        ).astype(F32)
        projected = jnp.dot(normalize(mine), weights_in, preferred_element_type=F32)
        for q in range(group):
            part = projected[q * tokens : (q + 1) * tokens]
            qkv_ref[first + q, :, :channels] = (part[:, :channels] * head_size ** (-0.5)).astype(BF16)
            qkv_ref[first + q, :, channels:] = part[:, channels : 3 * channels].astype(BF16)
            values = part[:, 2 * channels : 3 * channels].astype(BF16).astype(F32)
            even_ref[first + q] = jnp.mean(values, axis=0, keepdims=True)
            gate_ref[first + q] = jax.nn.sigmoid(part[:, 3 * channels :] + bg_ref[...])


def attend_kernel(
    info_ref, got_ref, qkv_ref, gate_ref, even_ref, wo_ref, bo_ref, *refs, far
):
    blocks, out_ref = refs[:-1], refs[-1]
    core, pair = info_ref[0], info_ref[1]
    earlier, blocks = (blocks[:2], blocks[2:]) if far == 2 else ((), blocks)
    rows, _, tile_rows, channels = got_ref.shape
    picks, tokens = qkv_ref.shape[:2]
    heads, width = blocks[0].shape[:2]
    head_size = channels // heads
    tiles = width // tile_rows
    half = 1 - pair if far else pair
    starts = []
    for n in range(len(blocks)):
        mine = core if (n == 0) == (far != 2) else 1 - core
        starts.append((half * 2 + mine) * width)
    lane_head = lax.broadcasted_iota(jnp.int32, (1, channels), 1) // head_size
    for n, start in enumerate(starts):
        at = pl.ds(pl.multiple_of(start, width), width)
        bias = blocks[n][...].reshape(heads * width, tokens).astype(F32)

        def product(q):
            some = qkv_ref[q, at, :channels]
            keys = qkv_ref[q, :, channels : 2 * channels]
            stacked = jnp.concatenate(
                [jnp.where(lane_head == h, some, jnp.zeros_like(some)) for h in range(heads)],
                axis=0,
            )
            return lax.dot_general(stacked, keys, CONTRACT_LAST, preferred_element_type=F32)

        def mixed(q, weights):
            values = qkv_ref[q, :, 2 * channels :]
            values_ones = jnp.concatenate([values, jnp.ones_like(values)], axis=1)
            both = jnp.dot(weights, values_ones, preferred_element_type=F32)
            top = total = None
            for h in range(heads):
                one = both[h * width : (h + 1) * width]
                if h == 0:
                    top, total = one[:, :channels], one[:, channels:]
                else:
                    top = jnp.where(lane_head == h, one[:, :channels], top)
                    total = jnp.where(lane_head == h, one[:, channels:], total)
            real = column_is_real(info_ref, q, rows, width)
            return gate_ref[q, at] * jnp.where(real, top / total, even_ref[q])

        attended = []
        following, weights = product(0), None
        for q in range(picks):
            scores = following + bias
            following = product(q + 1) if q + 1 < picks else None
            if q:
                attended.append(mixed(q - 1, weights))
            weights = jnp.exp(scores - jnp.max(scores, axis=1, keepdims=True)).astype(BF16)
        attended.append(mixed(picks - 1, weights))
        mix = jnp.concatenate(attended, axis=0).astype(BF16)
        update = jnp.dot(mix, wo_ref[...], preferred_element_type=F32) + bo_ref[...]
        for t in range(tiles):
            place = info_ref[4 + start // tile_rows + t]
            to = info_ref[4 + rows + start // tile_rows + t] if earlier else n * tiles + t
            for q in range(picks):
                change = update[q * width + t * tile_rows : q * width + (t + 1) * tile_rows]
                out_ref[to, q] = (got_ref[place, q].astype(F32) + change).astype(BF16)
    if earlier:
        near_ref, far_ref = earlier
        for part, first, half_of, mine in (
            (near_ref, 0, pair, core),
            (near_ref, tiles, pair, 1 - core),
            (far_ref, 0, half, core),
        ):
            for t in range(tiles):
                to = info_ref[4 + rows + (half_of * 2 + mine) * tiles + t]
                out_ref[to] = part[first + t]


def unpack_kernel(got_ref, out_ref):
    peers, picks = got_ref.shape[:2]
    for q in range(picks):
        columns = jnp.stack([got_ref[PLACE_BACK[row], q] for row in ORDER], axis=0)
        out_ref[:, q * peers : (q + 1) * peers] = jnp.swapaxes(columns, 0, 1)


def call(kernel, name, out, *operands, cost, vmem=28, scratch=(), **grid):
    grid.setdefault("in_specs", [SCALARS if o.ndim == 1 else WHOLE for o in operands])
    grid.setdefault("out_specs", jax.tree.map(lambda _: WHOLE, out))
    return pl.pallas_call(
        kernel,
        out_shape=out,
        scratch_shapes=list(scratch),
        compiler_params=pltpu.CompilerParams(vmem_limit_bytes=vmem << 20),
        cost_estimate=pl.CostEstimate(flops=cost, bytes_accessed=0, transcendentals=0),
        name=name,
        **grid,
    )(*operands)


def local(pair_state, valid_tokens, w_query, w_key, w_value, w_gate, b_gate, w_bias, w_out, b_out):
    tile_rows, tile_cols, channels = pair_state.shape
    heads = w_bias.shape[1]
    peers = lax.axis_size("row")
    picks = tile_cols // peers
    tokens = peers * tile_rows
    places = jnp.array(PLACE + PLACE_BACK, jnp.int32)
    here = [lax.axis_index("core"), lax.axis_index("xl"), places[lax.axis_index("row")]]
    info = jnp.concatenate([jnp.stack(here + [valid_tokens[0]]).astype(jnp.int32), places])
    of = jax.ShapeDtypeStruct
    swap = [(0, 1), (1, 0)]

    def exchange(array, order):
        return lax.all_to_all(array, "row", 0, 0, axis_index_groups=[list(order)], tiled=True)

    part = tile_rows // 2
    slots = picks + heads
    sent = call(
        pack_kernel, "pack", of((peers, slots, tile_rows, channels), BF16), pair_state, w_bias.T,
        grid=(2,),
        in_specs=[
            pl.BlockSpec((part, tile_cols, channels), lambda a: (a, 0, 0)),
            pl.BlockSpec((heads, channels), lambda a: (0, 0)),
        ],
        out_specs=pl.BlockSpec((peers, slots, part, channels), lambda a: (0, 0, a, 0)),
        cost=4 * MICROSECOND, vmem=62,
    )
    got = exchange(sent, ORDER)
    own = call(bias_kernel, "turn_bias", of((heads, tile_cols, tokens), BF16), info, got, cost=MICROSECOND)
    far = lax.ppermute(own, "xl", swap)
    near = lax.ppermute(own, "core", swap)
    qkv, gate, even = call(
        functools.partial(project_kernel, head_size=channels // heads), "project",
        (
            of((picks, tokens, 3 * channels), BF16), of((picks, tokens, channels), F32),
            of((picks, 1, channels), F32),
        ),
        info, got, w_query, w_key, w_value, w_gate, b_gate[None],
        cost=3 * MICROSECOND,
    )

    def attend(name, far, *blocks, earlier=()):
        count = len(blocks)
        tiles = peers if earlier else count * tile_cols // tile_rows
        return call(
            functools.partial(attend_kernel, far=far), name,
            of((tiles, picks, tile_rows, channels), BF16),
            info, got, qkv, gate, even, w_out, b_out[None], *earlier, *blocks,
            cost=3 * count * MICROSECOND,
        )

    first = attend("attend_near", 0, own, near)
    far, first = lax.optimization_barrier((far, first))
    last = lax.ppermute(far, "core", swap)
    second = attend("attend_far", 1, far)
    done = attend("attend_last", 2, last, earlier=(first, second))
    back = exchange(done, ORDER_BACK)
    return call(unpack_kernel, "unpack", of(pair_state.shape, BF16), back, cost=MICROSECOND)


def solution(mesh):
    crops, rows, cols = (mesh.shape[name] for name in ("crop", "row", "col"))
    split = Mesh(
        mesh.devices.reshape(crops, rows, cols // 2, 2), ("crop", "row", "xl", "core")
    )
    return jax.shard_map(
        local,
        mesh=split,
        in_specs=(P(("crop", "row"), ("xl", "core"), None), P("crop")) + (P(),) * 8,
        out_specs=P(("crop", "row"), ("xl", "core"), None),
        check_vma=False,
    )
```

```python
import functools

import jax
import jax.numpy as jnp
from jax import lax
from jax.experimental import pallas as pl
from jax.experimental.pallas import tpu as pltpu
from jax.sharding import Mesh
from jax.sharding import PartitionSpec as P

F32 = jnp.float32
BF16 = jnp.bfloat16
MASKED_SCORE = -1000000000.0
CONTRACT_LAST = (((1,), (1,)), ((), ()))
MICROSECOND = 1_150_000_000
ORDER = (10, 5, 0, 1, 9, 4, 6, 2, 3, 15, 11, 7, 12, 8, 13, 14)
ORDER_BACK = (10, 14, 5, 1, 9, 2, 3, 11, 13, 7, 8, 4, 0, 6, 15, 12)
PLACE = tuple(ORDER.index(row) for row in range(len(ORDER)))
PLACE_BACK = tuple(ORDER_BACK.index(row) for row in range(len(ORDER)))
WHOLE = pl.BlockSpec(memory_space=pltpu.VMEM)
SCALARS = pl.BlockSpec(memory_space=pltpu.SMEM)


def normalize(floats):
    average = jnp.mean(floats, axis=-1, keepdims=True)
    centered = floats - average
    variance = jnp.mean(centered * centered, axis=-1, keepdims=True)
    return (centered * lax.rsqrt(variance + 1e-05)).astype(BF16)


def pack_kernel(x_ref, wb_ref, out_ref):
    rows = x_ref.shape[0]
    peers, slots = out_ref.shape[:2]
    heads = wb_ref.shape[0]
    picks = slots - heads
    cols = x_ref.shape[1]
    normed = normalize(x_ref[...].reshape(rows * cols, -1).astype(F32))
    bias = lax.dot_general(wb_ref[...], normed, CONTRACT_LAST, preferred_element_type=F32)
    bias = jnp.stack([bias[:, r * cols : (r + 1) * cols] for r in range(rows)], axis=1)
    bias = bias.astype(BF16)
    for d in range(peers):
        out_ref[d, picks:] = bias
    turned = jnp.swapaxes(x_ref[...], 0, 1)
    for q in range(picks):
        out_ref[:, q] = turned[q * peers : (q + 1) * peers]


def bias_kernel(info_ref, got_ref, out_ref):
    heads, width, tokens = out_ref.shape
    first = got_ref.shape[1] - heads
    key_ok = lax.broadcasted_iota(jnp.int32, (1, tokens), 1) < info_ref[3]
    for h in range(heads):
        block = jnp.transpose(jnp.concatenate([got_ref[at, first + h] for at in PLACE], axis=0))
        out_ref[h] = jnp.where(key_ok, block.astype(F32), MASKED_SCORE).astype(BF16)


def column_is_real(info_ref, q, peers, width):
    column = (info_ref[1] * 2 + info_ref[0]) * width + q * peers + info_ref[2]
    return column < info_ref[3]


def project_kernel(
    info_ref, got_ref, wq_ref, wk_ref, wv_ref, wg_ref, bg_ref, qkv_ref, gate_ref, even_ref, *,
    head_size
):
    rows, _, tile_rows, channels = got_ref.shape
    picks, tokens = qkv_ref.shape[:2]
    group = picks // 2
    weights_in = jnp.concatenate([wq_ref[...], wk_ref[...], wv_ref[...], wg_ref[...]], axis=1)
    for first in range(0, picks, group):
        mine = jnp.concatenate(
            [got_ref[at, first + q] for q in range(group) for at in PLACE], axis=0
        ).astype(F32)
        projected = jnp.dot(normalize(mine), weights_in, preferred_element_type=F32)
        for q in range(group):
            part = projected[q * tokens : (q + 1) * tokens]
            qkv_ref[first + q, :, :channels] = (part[:, :channels] * head_size ** (-0.5)).astype(BF16)
            qkv_ref[first + q, :, channels:] = part[:, channels : 3 * channels].astype(BF16)
            values = part[:, 2 * channels : 3 * channels].astype(BF16).astype(F32)
            even_ref[first + q] = jnp.mean(values, axis=0, keepdims=True)
            gate_ref[first + q] = jax.nn.sigmoid(part[:, 3 * channels :] + bg_ref[...])


def attend_kernel(
    info_ref, got_ref, qkv_ref, gate_ref, even_ref, wo_ref, bo_ref, *refs, far
):
    blocks, out_ref = refs[:-1], refs[-1]
    core, pair = info_ref[0], info_ref[1]
    earlier, blocks = (blocks[:2], blocks[2:]) if far == 2 else ((), blocks)
    rows, _, tile_rows, channels = got_ref.shape
    picks, tokens = qkv_ref.shape[:2]
    heads, width = blocks[0].shape[:2]
    head_size = channels // heads
    tiles = width // tile_rows
    half = 1 - pair if far else pair
    starts = []
    for n in range(len(blocks)):
        mine = core if (n == 0) == (far != 2) else 1 - core
        starts.append((half * 2 + mine) * width)
    lane_head = lax.broadcasted_iota(jnp.int32, (1, channels), 1) // head_size
    for n, start in enumerate(starts):
        at = pl.ds(pl.multiple_of(start, width), width)
        bias = blocks[n][...].reshape(heads * width, tokens).astype(F32)

        def product(q):
            some = qkv_ref[q, at, :channels]
            keys = qkv_ref[q, :, channels : 2 * channels]
            stacked = jnp.concatenate(
                [jnp.where(lane_head == h, some, jnp.zeros_like(some)) for h in range(heads)],
                axis=0,
            )
            return lax.dot_general(stacked, keys, CONTRACT_LAST, preferred_element_type=F32)

        def mixed(q, weights):
            values = qkv_ref[q, :, 2 * channels :]
            values_ones = jnp.concatenate([values, jnp.ones_like(values)], axis=1)
            both = jnp.dot(weights, values_ones, preferred_element_type=F32)
            top = total = None
            for h in range(heads):
                one = both[h * width : (h + 1) * width]
                if h == 0:
                    top, total = one[:, :channels], one[:, channels:]
                else:
                    top = jnp.where(lane_head == h, one[:, :channels], top)
                    total = jnp.where(lane_head == h, one[:, channels:], total)
            real = column_is_real(info_ref, q, rows, width)
            return gate_ref[q, at] * jnp.where(real, top / total, even_ref[q])

        attended = []
        following, weights = product(0), None
        for q in range(picks):
            scores = following + bias
            following = product(q + 1) if q + 1 < picks else None
            if q:
                attended.append(mixed(q - 1, weights))
            weights = jnp.exp(scores - jnp.max(scores, axis=1, keepdims=True)).astype(BF16)
        attended.append(mixed(picks - 1, weights))
        mix = jnp.concatenate(attended, axis=0).astype(BF16)
        update = jnp.dot(mix, wo_ref[...], preferred_element_type=F32) + bo_ref[...]
        for t in range(tiles):
            place = info_ref[4 + start // tile_rows + t]
            to = info_ref[4 + rows + start // tile_rows + t] if earlier else n * tiles + t
            for q in range(picks):
                change = update[q * width + t * tile_rows : q * width + (t + 1) * tile_rows]
                out_ref[to, q] = (got_ref[place, q].astype(F32) + change).astype(BF16)
    if earlier:
        near_ref, far_ref = earlier
        for part, first, half_of, mine in (
            (near_ref, 0, pair, core),
            (near_ref, tiles, pair, 1 - core),
            (far_ref, 0, half, core),
        ):
            for t in range(tiles):
                to = info_ref[4 + rows + (half_of * 2 + mine) * tiles + t]
                out_ref[to] = part[first + t]


def unpack_kernel(got_ref, out_ref):
    peers, picks = got_ref.shape[:2]
    for q in range(picks):
        columns = jnp.stack([got_ref[PLACE_BACK[row], q] for row in ORDER], axis=0)
        out_ref[:, q * peers : (q + 1) * peers] = jnp.swapaxes(columns, 0, 1)


def call(kernel, name, out, *operands, cost, vmem=28, scratch=(), **grid):
    grid.setdefault("in_specs", [SCALARS if o.ndim == 1 else WHOLE for o in operands])
    grid.setdefault("out_specs", jax.tree.map(lambda _: WHOLE, out))
    return pl.pallas_call(
        kernel,
        out_shape=out,
        scratch_shapes=list(scratch),
        compiler_params=pltpu.CompilerParams(vmem_limit_bytes=vmem << 20),
        cost_estimate=pl.CostEstimate(flops=cost, bytes_accessed=0, transcendentals=0),
        name=name,
        **grid,
    )(*operands)


def local(pair_state, valid_tokens, w_query, w_key, w_value, w_gate, b_gate, w_bias, w_out, b_out):
    tile_rows, tile_cols, channels = pair_state.shape
    heads = w_bias.shape[1]
    peers = lax.axis_size("row")
    picks = tile_cols // peers
    tokens = peers * tile_rows
    places = jnp.array(PLACE + PLACE_BACK, jnp.int32)
    here = [lax.axis_index("core"), lax.axis_index("xl"), places[lax.axis_index("row")]]
    info = jnp.concatenate([jnp.stack(here + [valid_tokens[0]]).astype(jnp.int32), places])
    of = jax.ShapeDtypeStruct
    swap = [(0, 1), (1, 0)]

    def exchange(array, order):
        return lax.all_to_all(array, "row", 0, 0, axis_index_groups=[list(order)], tiled=True)

    part = tile_rows // 2
    slots = picks + heads
    sent = call(
        pack_kernel, "pack", of((peers, slots, tile_rows, channels), BF16), pair_state, w_bias.T,
        grid=(2,),
        in_specs=[
            pl.BlockSpec((part, tile_cols, channels), lambda a: (a, 0, 0)),
            pl.BlockSpec((heads, channels), lambda a: (0, 0)),
        ],
        out_specs=pl.BlockSpec((peers, slots, part, channels), lambda a: (0, 0, a, 0)),
        cost=4 * MICROSECOND, vmem=62,
    )
    got = exchange(sent, ORDER)
    own = call(bias_kernel, "turn_bias", of((heads, tile_cols, tokens), BF16), info, got, cost=MICROSECOND)
    far = lax.ppermute(own, "xl", swap)
    near = lax.ppermute(own, "core", swap)
    qkv, gate, even = call(
        functools.partial(project_kernel, head_size=channels // heads), "project",
        (
            of((picks, tokens, 3 * channels), BF16), of((picks, tokens, channels), F32),
            of((picks, 1, channels), F32),
        ),
        info, got, w_query, w_key, w_value, w_gate, b_gate[None],
        cost=3 * MICROSECOND,
    )

    def attend(name, far, *blocks, earlier=()):
        count = len(blocks)
        tiles = peers if earlier else count * tile_cols // tile_rows
        return call(
            functools.partial(attend_kernel, far=far), name,
            of((tiles, picks, tile_rows, channels), BF16),
            info, got, qkv, gate, even, w_out, b_out[None], *earlier, *blocks,
            cost=3 * count * MICROSECOND,
        )

    first = attend("attend_near", 0, own, near)
    far, first = lax.optimization_barrier((far, first))
    last = lax.ppermute(far, "core", swap)
    second = attend("attend_far", 1, far)
    done = attend("attend_last", 2, last, earlier=(first, second))
    back = exchange(done, ORDER_BACK)
    return call(
        unpack_kernel, "unpack", of(pair_state.shape, BF16), back,
        grid=(2,),
        in_specs=[pl.BlockSpec((peers, picks, part, channels), lambda a: (0, 0, a, 0))],
        out_specs=pl.BlockSpec((part, tile_cols, channels), lambda a: (a, 0, 0)),
        cost=MICROSECOND,
    )


def solution(mesh):
    crops, rows, cols = (mesh.shape[name] for name in ("crop", "row", "col"))
    split = Mesh(
        mesh.devices.reshape(crops, rows, cols // 2, 2), ("crop", "row", "xl", "core")
    )
    return jax.shard_map(
        local,
        mesh=split,
        in_specs=(P(("crop", "row"), ("xl", "core"), None), P("crop")) + (P(),) * 8,
        out_specs=P(("crop", "row"), ("xl", "core"), None),
        check_vma=False,
    )
```
